32 devices in a mesh: groups: 2 (over y), dp: 4 (over z), tensor: 4 (over x, core).
Axes of the slice: x: 2, y: 2, z: 4, core: 2. Of those that a mesh axis runs over, the one named last changes fastest.
Arguments:
- x_inner: bfloat16 [2048, 8192], P(('groups', 'dp'), 'tensor'), parts along dimension 0, may hold values from -6 to 6
- log_decay: float32 [2048, 128], P(('groups', 'dp'), 'tensor'), parts along dimension 0, may hold values from -2.5 to 0, as said below
- in_map: float32 [2048, 16], P(('groups', 'dp')), parts along dimension 0, may hold values from -6 to 6
- out_map: float32 [2048, 16], P(('groups', 'dp')), parts along dimension 0, may hold values from -0.125 to 0.125
- grad_out: bfloat16 [2048, 8192], P(('groups', 'dp'), 'tensor'), parts along dimension 0, may hold values from -6 to 6
Outputs:
- scan_out: bfloat16 [2048, 8192], P(('groups', 'dp'), 'tensor'), parts along dimension 0
- grad_inner: bfloat16 [2048, 8192], P(('groups', 'dp'), 'tensor'), parts along dimension 0
- grad_decay: float32 [2048, 128], P(('groups', 'dp'), 'tensor'), parts along dimension 0
- grad_in_map: float32 [2048, 16], P(('groups', 'dp')), parts along dimension 0
- output_map_gradient: float32 [2048, 16], P(('groups', 'dp')), parts along dimension 0
The draws below stay inside these ranges and needn't reach their ends.
There are 2 independent parts, one for each index of `groups`. The reference program is written for one: setup_inputs(seed, part) draws one part's arguments, and reference() takes and returns one part's arrays. A program takes and returns all parts, laid end to end along the dimension named above; each array names one. Nothing has to cross between parts.
Inputs may be any that keep to these rules, and one draw needn't show every extreme that they name: log_decay is negative.
All inputs are finite; a program needn't handle non-finite values.
Results may differ from the reference program's by a relative error of at most 0.012.
Values sent between devices are 32-bit elements; how exact they have to be, the bound alone decides.
A program may use at most 128 MiB of HBM per device.

```python
import jax
import jax.numpy as jnp
from jax import lax

HEADS = 128
HEAD_SIZE = 64
STATE = 16
BLOCK = 128
TOKENS = 1024


def draw_log_decay(key, part):
    key = jax.random.fold_in(key, 11)
    keys = jax.random.split(key, 6)
    slow_share = 0.5
    slow_heads = jax.random.uniform(keys[0], (HEADS,)) < slow_share
    slow_rate = jax.random.uniform(keys[1], (HEADS,), minval=0.2, maxval=0.6) / TOKENS
    fast_rate = jnp.exp(jax.random.uniform(keys[2], (HEADS,), minval=jnp.log(0.02), maxval=jnp.log(0.1)))
    baseline_decay_rate = jnp.where(slow_heads, slow_rate, fast_rate)
    coarse_estimate = jnp.exp(jax.random.uniform(keys[3], (TOKENS, HEADS), minval=-0.69, maxval=0.69))
    positions = jax.random.randint(keys[4], (3, HEADS), 0, TOKENS)
    layer_stack_depth = jax.random.uniform(keys[5], (3, HEADS), minval=0.23, maxval=0.69)
    boundary_markers = (jnp.arange(TOKENS)[None, :, None] == positions[:, None, :]).astype(jnp.float32)
    spike_events = jnp.sum(boundary_markers * layer_stack_depth[:, None, :], axis=0)
    return -(baseline_decay_rate[None, :] * coarse_estimate + spike_events)


def level_of(rng, shape, cuts, smallest, high):
    def one(dim, shards_of):
        heights = jax.random.uniform(jax.random.fold_in(jax.random.fold_in(rng, 6), dim), (shards_of,), jnp.float32, smallest / len(cuts), high / len(cuts))
        return jnp.repeat(jnp.exp(heights), shape[dim] // shards_of).reshape((-1,) + (1,) * (len(shape) - dim - 1))

    gain = one(*cuts[0])
    for cut in cuts[1:]:
        gain = gain * one(*cut)
    return gain


def noise(rng, shape, width, reach, shards=(), dtype=jnp.bfloat16):
    factor_of = level_of(rng, shape, shards, -0.22, 0.18) if shards else 1.0
    array = jax.random.normal(rng, shape, jnp.float32) * width * factor_of
    return jnp.minimum(jnp.maximum(array, -reach), reach).astype(dtype)


def setup_inputs(seed: int = 0, part: int = 0) -> dict:
    arg_keys = jax.random.split(jax.random.key(seed), 6)
    own_keys = jax.random.split(jax.random.fold_in(arg_keys[5], part), 6)
    x_inner = noise(own_keys[0], (TOKENS, HEADS * HEAD_SIZE), 1.0, 6.0, ((0, 4), (1, 4)))
    log_decay = draw_log_decay(jax.random.fold_in(jax.random.fold_in(arg_keys[5], part), 71), part)
    in_map = noise(own_keys[2], (TOKENS, STATE), 1.0, 6.0, ((0, 4),), jnp.float32)
    out_map = noise(own_keys[3], (TOKENS, STATE), (0.25 / TOKENS ** 0.5), 0.125, ((0, 4),), jnp.float32)
    grad_out = noise(own_keys[4], (TOKENS, HEADS * HEAD_SIZE), 1.0, 6.0, ((0, 4), (1, 4)))
    return {"x_inner": x_inner, "log_decay": log_decay, "in_map": in_map, "out_map": out_map, "grad_out": grad_out}


def block_pass(carry_state, pieces):
    inputs, decays, in_rows, out_rows = pieces
    cumulative = jnp.cumsum(decays, axis=0)
    length = decays.shape[0]
    causal = jnp.arange(length)[:, None] >= jnp.arange(length)[None, :]
    by_head = cumulative.T
    spread = by_head[:, :, None] - by_head[:, None, :]
    weights = jnp.exp(jnp.where(causal[None, :, :], spread, -1e+30))
    scores = jnp.dot(out_rows, in_rows.T, preferred_element_type=jnp.float32, precision=lax.Precision.HIGHEST)
    mixing = weights * scores[None, :, :]
    within = jnp.einsum('hts,shp->thp', mixing, inputs, preferred_element_type=jnp.float32)
    carried = jnp.exp(cumulative)[:, :, None] * jnp.einsum('tn,hpn->thp', out_rows, carry_state, preferred_element_type=jnp.float32)
    tail_decay = jnp.exp(cumulative[-1][None, :] - cumulative)
    new_state = jnp.exp(cumulative[-1])[:, None, None] * carry_state + jnp.einsum('sh,shp,sn->hpn', tail_decay, inputs, in_rows, preferred_element_type=jnp.float32)
    return (new_state, within + carried)

def run_rows(inputs, decays, in_rows, out_rows, carry_state, block_len):
    row_count = inputs.shape[0]
    head_count = decays.shape[1]
    head_width = carry_state.shape[1]
    count_of_blocks = row_count // block_len
    pieces = (inputs.reshape(count_of_blocks, block_len, head_count, head_width), decays.reshape(count_of_blocks, block_len, head_count), in_rows.reshape(count_of_blocks, block_len, -1), out_rows.reshape(count_of_blocks, block_len, -1))
    last_state, outputs = lax.scan(jax.checkpoint(block_pass), carry_state, pieces)
    return (outputs.reshape(row_count, head_count * head_width), last_state)

def reference(x_inner, log_decay, in_map, out_map, grad_out):
    head_count = log_decay.shape[1]
    zero_state = jnp.zeros((head_count, HEAD_SIZE, STATE), jnp.float32)

    def forward(inputs, decays, in_rows, out_rows):
        return run_rows(inputs, decays, in_rows, out_rows, zero_state, BLOCK)
    primal = (x_inner.astype(jnp.float32), log_decay, in_map, out_map)
    (outputs, last_state), pullback = jax.vjp(forward, *primal)
    gradients = pullback((grad_out.astype(jnp.float32), jnp.zeros_like(last_state)))
    return (outputs.astype(jnp.bfloat16), gradients[0].astype(jnp.bfloat16), gradients[1], gradients[2], gradients[3])
```

```python
import functools

import jax
import jax.numpy as jnp
from jax import lax
from jax.experimental import pallas as pl
from jax.experimental.pallas import tpu as pltpu
from jax.sharding import PartitionSpec as P

F32 = jnp.float32
BF16 = jnp.bfloat16
L = 128
PIECES = 4
MESH = pl.DeviceIdType.MESH
HI = lax.Precision.HIGHEST
NN = (((1,), (0,)), ((), ()))
NT = (((1,), (1,)), ((), ()))
TN = (((0,), (0,)), ((), ()))


def dot(a, b, dims=NN, precision=None):
    return lax.dot_general(a, b, dims, precision=precision, preferred_element_type=F32)


def split(a, terms):
    parts = []
    for _ in range(terms):
        part = a.astype(BF16)
        parts.append(part)
        a = a - part.astype(F32)
    return parts


def exact_right(a, ones, dims=NN, terms=3):
    return sum(dot(part, ones, dims) for part in split(a, terms))


def exact_left(ones, a, dims=NN, terms=3):
    return sum(dot(ones, part, dims) for part in split(a, terms))


def iota(shape, dim):
    return lax.broadcasted_iota(jnp.int32, shape, dim)


def ones_where(cond):
    return jnp.where(cond, 1.0, 0.0).astype(BF16)


def kernel(
    hops, peers, heads, x_ref, ld_ref, b_ref, c_ref, g_ref,
    y_ref, dx_ref, gd_ref, d_in_ref, d_out_ref,
    ys, dxs, own, gown, fin, fout, gin, gout, sbd, gbd, pex, mall,
    fsend, frecv, bsend, brecv, msend, mrecv,
):
    rows, width = x_ref.shape
    state = b_ref.shape[0]
    head = width // heads
    chunks = rows // L
    per = heads // PIECES
    wide = per * head
    place = lax.axis_index("dp")
    mine = lax.axis_index("tensor")

    barrier = pltpu.get_barrier_semaphore()
    for d in range(1, peers):
        pl.semaphore_signal(
            barrier, inc=1, device_id={"tensor": lax.rem(mine + d, peers)}, device_id_type=MESH
        )

    @pl.when(place > 0)
    def _():
        pl.semaphore_signal(barrier, inc=1, device_id={"dp": place - 1}, device_id_type=MESH)

    @pl.when(place < hops - 1)
    def _():
        pl.semaphore_signal(barrier, inc=1, device_id={"dp": place + 1}, device_id_type=MESH)

    causal = iota((L, L), 0) >= iota((L, L), 1)
    tril = ones_where(causal)
    upper = ones_where(iota((L, L), 0) <= iota((L, L), 1))
    by_col = ones_where(iota((heads, width), 0) == iota((heads, width), 1) // head)
    by_state = ones_where(iota((heads, heads * state), 0) == iota((heads, heads * state), 1) // state)
    tile = ones_where(iota((state, per * state), 0) == iota((state, per * state), 1) % state)
    quad = 4 * head

    cum, cum_t, e_exp, t_exp, ce, be, b_t, c_t = [], [], [], [], [], [], [], []
    for c in range(chunks):
        at = pl.ds(c * L, L)
        cu = exact_left(tril, ld_ref[:, at], NT)
        cut = exact_right(ld_ref[:, at], upper)
        cum.append(cu)
        cum_t.append(cut)
        bt = b_ref[:, at]
        ct = c_ref[:, at]
        b_t.append(bt)
        c_t.append(ct)
        pex[c] = jnp.exp(exact_right(cu[L - 8:, :], by_col))
        et = jnp.exp(cut)
        tt = jnp.exp(cut[:, L - 1:] - cut)
        for k in range(width // quad):
            lanes = pl.ds(k * quad, quad)
            lhs_b = jnp.concatenate([bt * tt[h:h + 1, :] for h in range(4 * k, 4 * k + 4)], 0).astype(BF16)
            lhs_c = jnp.concatenate([ct * et[h:h + 1, :] for h in range(4 * k, 4 * k + 4)], 0).astype(BF16)
            rb = dot(lhs_b, x_ref[at, lanes])
            rc = dot(lhs_c, g_ref[at, lanes])
            which = iota((state, quad), 1) // head
            ob = rb[:state]
            oc = rc[:state]
            for h in range(1, 4):
                ob = jnp.where(which == h, rb[h * state:(h + 1) * state], ob)
                oc = jnp.where(which == h, rc[h * state:(h + 1) * state], oc)
            own[c, k * quad // wide, :, (k * quad) % wide:(k * quad) % wide + quad] = ob
            gown[c, k * quad // wide, :, (k * quad) % wide:(k * quad) % wide + quad] = oc

    pl.semaphore_wait(
        barrier, peers - 1 + jnp.minimum(place, 1) + jnp.minimum(hops - 1 - place, 1)
    )

    def decay(c, k):
        return pex[c, 7:8, k * wide:(k + 1) * wide]

    def f_copy(k):
        return pltpu.make_async_remote_copy(
            src_ref=fout.at[k], dst_ref=fin.at[k], send_sem=fsend.at[k], recv_sem=frecv.at[k],
            device_id={"dp": place + 1}, device_id_type=MESH,
        )

    def b_copy(k):
        return pltpu.make_async_remote_copy(
            src_ref=gout.at[k], dst_ref=gin.at[k], send_sem=bsend.at[k], recv_sem=brecv.at[k],
            device_id={"dp": place - 1}, device_id_type=MESH,
        )

    def relay(first):
        for k in range(PIECES):
            @pl.when(place == 0 if first else place > 0)
            def _():
                if first:
                    fin[k] = jnp.zeros(fin.shape[1:], F32)
                else:
                    f_copy(k).wait_recv()

            @pl.when(place < hops - 1)
            def _():
                s = own[0, k] if first else decay(0, k) * fin[k] + own[0, k]
                for c in range(1, chunks):
                    s = decay(c, k) * s + own[c, k]
                fout[k] = s
                f_copy(k).start()

    def relay_back(first):
        for k in range(PIECES):
            @pl.when(place == hops - 1 if first else place < hops - 1)
            def _():
                if first:
                    gin[k] = jnp.zeros(gin.shape[1:], F32)
                else:
                    b_copy(k).wait_recv()

            @pl.when(place > 0)
            def _():
                last = chunks - 1
                s = gown[last, k] if first else decay(last, k) * gin[k] + gown[last, k]
                for c in range(chunks - 2, -1, -1):
                    s = decay(c, k) * s + gown[c, k]
                gout[k] = s
                b_copy(k).start()

    stages = min(hops, 4)
    from_end = hops - 1 - place

    def exchange(stage):
        when = (lambda v: v >= stage) if stage == stages - 1 else (lambda v: v == stage)

        @pl.when(when(place))
        def _():
            relay(stage == 0)

        @pl.when(when(from_end))
        def _():
            relay_back(stage == 0)

    exchange(0)

    scores, grad_scores = [], []
    for c in range(chunks):
        at = pl.ds(c * L, L)
        s = dot(c_t[c], b_t[c], TN, HI)
        scores.append(jnp.where(causal, s, 0.0))
        grad_scores.append(jnp.zeros((L, L), F32))
        ct8 = exact_right(c_t[c], tile, TN)
        bt8 = exact_right(b_t[c], tile, TN)
        cue = exact_right(cum[c], by_state)
        ee = jnp.exp(cue)
        te = jnp.exp(cue[L - 1:, :] - cue)
        e_exp.append(ee)
        t_exp.append(te)
        lanes = per * state
        ce.append([(ct8 * ee[:, k * lanes:(k + 1) * lanes]).astype(BF16) for k in range(PIECES)])
        be.append([(bt8 * te[:, k * lanes:(k + 1) * lanes]).astype(BF16) for k in range(PIECES)])

    pair = 2 * head
    left = ones_where(iota((L, pair), 1) < head)
    right = ones_where(iota((L, pair), 1) >= head)
    units = [(c, p) for p in range(width // pair) for c in range(chunks)]
    for n, (c, p) in enumerate(units):
        for stage in range(1, stages):
            if n == len(units) * stage // (stages - 1) - 1 and stage < stages - 1:
                exchange(stage)
        at = pl.ds(c * L, L)
        lanes = pl.ds(p * pair, pair)
        weights = []
        for h in (2 * p, 2 * p + 1):
            diff = cum[c][:, h:h + 1] - cum_t[c][h:h + 1, :]
            weights.append(jnp.exp(jnp.minimum(diff, 0.0)))
        mix = [(w * scores[c]).astype(BF16) for w in weights]
        x = x_ref[at, lanes]
        g = g_ref[at, lanes]
        x2 = jnp.concatenate([x * left, x * right], 0)
        g2 = jnp.concatenate([g * left, g * right], 0)
        ys[at, lanes] = dot(jnp.concatenate(mix, 1), x2)
        dxs[at, lanes] = dot(jnp.concatenate(mix, 0), g2, TN)
        dm = dot(g, x2, NT)
        grad_scores[c] += weights[0] * dm[:, :L] + weights[1] * dm[:, L:]
    if stages > 1:
        exchange(stages - 1)

    block = ones_where(iota((per * state, wide), 0) // state == iota((per * state, wide), 1) // head)
    acc_c = [jnp.zeros((L, per * state), F32) for _ in range(chunks)]
    acc_b = [jnp.zeros((L, per * state), F32) for _ in range(chunks)]
    ends = []
    for k in range(PIECES):
        states = [fin[k]]
        for c in range(chunks):
            states.append(decay(c, k) * states[c] + own[c, k])
        grads = [gin[k]]
        for c in range(chunks - 1, 0, -1):
            grads.append(decay(c, k) * grads[-1] + gown[c, k])
        grads = grads[::-1]
        ends.append([jnp.sum(grads[c] * states[c + 1], 0, keepdims=True) for c in range(chunks)])
        for c in range(chunks):
            at = pl.ds(c * L, L)
            cols = pl.ds(k * wide, wide)
            lanes = slice(k * per * state, (k + 1) * per * state)
            s2 = jnp.concatenate([states[c].astype(BF16)] * per, 0) * block
            r2 = jnp.concatenate([grads[c].astype(BF16)] * per, 0) * block
            sbd[c, k] = s2
            gbd[c, k] = r2
            acc_c[c] += dot(g_ref[at, cols], s2, NT) * e_exp[c][:, lanes]
            acc_b[c] += dot(x_ref[at, cols], r2, NT) * t_exp[c][:, lanes]

    for c in range(chunks):
        ds = jnp.where(causal, grad_scores[c], 0.0)
        mall[mine, :state, c * L:(c + 1) * L] = exact_left(tile, acc_c[c], NT) + dot(b_t[c], ds, NT, HI)
        mall[mine, state:, c * L:(c + 1) * L] = exact_left(tile, acc_b[c], NT) + dot(c_t[c], ds, NN, HI)

    def m_copy(d, slot):
        return pltpu.make_async_remote_copy(
            src_ref=mall.at[mine], dst_ref=mall.at[slot], send_sem=msend.at[d - 1], recv_sem=mrecv.at[d - 1],
            device_id={"tensor": lax.rem(mine + d, peers)}, device_id_type=MESH,
        )

    for d in range(1, peers):
        m_copy(d, mine).start()

    for c in range(chunks):
        at = pl.ds(c * L, L)
        dcum = jnp.zeros((heads, L), F32)
        for k in range(PIECES):
            cols = pl.ds(k * wide, wide)
            y = ys[at, cols] + dot(ce[c][k], sbd[c, k])
            dx = dxs[at, cols] + dot(be[c][k], gbd[c, k])
            y_ref[at, cols] = y.astype(BF16)
            dx_ref[at, cols] = dx.astype(BF16)
            q = g_ref[at, cols].astype(F32) * y - x_ref[at, cols].astype(F32) * dx
            q += jnp.where(iota((L, wide), 0) == L - 1, ends[k][c], 0.0)
            dcum += exact_left(by_col[:, k * wide:(k + 1) * wide], q, NT, 2)
        gd_ref[:, at] = exact_right(dcum, tril)

    for d in range(1, peers):
        m_copy(d, lax.rem(mine + peers - d, peers)).wait_recv()
        m_copy(d, mine).wait_send()
    total = mall[0]
    for d in range(1, peers):
        total += mall[d]
    d_out_ref[...] = total[:state]
    d_in_ref[...] = total[state:]

    @pl.when(place < hops - 1)
    def _():
        for k in range(PIECES):
            f_copy(k).wait_send()

    @pl.when(place > 0)
    def _():
        for k in range(PIECES):
            b_copy(k).wait_send()


def local(hops, peers, x_inner, log_decay, in_map, out_map, grad_out):
    rows, width = x_inner.shape
    heads = log_decay.shape[1]
    state = in_map.shape[1]
    chunks = rows // L
    wide = width // PIECES
    piece = (PIECES, state, wide)
    vm = pl.BlockSpec(memory_space=pltpu.VMEM)
    y, dx, gd, d_in, d_out = pl.pallas_call(
        functools.partial(kernel, hops, peers, heads),
        out_shape=(
            jax.ShapeDtypeStruct((rows, width), BF16),
            jax.ShapeDtypeStruct((rows, width), BF16),
            jax.ShapeDtypeStruct((heads, rows), F32),
            jax.ShapeDtypeStruct((state, rows), F32),
            jax.ShapeDtypeStruct((state, rows), F32),
        ),
        in_specs=[vm] * 5,
        out_specs=(vm,) * 5,
        scratch_shapes=[
            pltpu.VMEM((rows, width), F32),
            pltpu.VMEM((rows, width), F32),
            pltpu.VMEM((chunks,) + piece, F32),
            pltpu.VMEM((chunks,) + piece, F32),
            pltpu.VMEM(piece, F32),
            pltpu.VMEM(piece, F32),
            pltpu.VMEM(piece, F32),
            pltpu.VMEM(piece, F32),
            pltpu.VMEM((chunks, PIECES, heads // PIECES * state, wide), BF16),
            pltpu.VMEM((chunks, PIECES, heads // PIECES * state, wide), BF16),
            pltpu.VMEM((chunks, 8, width), F32),
            pltpu.VMEM((peers, 2 * state, rows), F32),
            pltpu.SemaphoreType.DMA((PIECES,)),
            pltpu.SemaphoreType.DMA((PIECES,)),
            pltpu.SemaphoreType.DMA((PIECES,)),
            pltpu.SemaphoreType.DMA((PIECES,)),
            pltpu.SemaphoreType.DMA((peers - 1,)),
            pltpu.SemaphoreType.DMA((peers - 1,)),
        ],
        compiler_params=pltpu.CompilerParams(
            collective_id=0, has_side_effects=True, vmem_limit_bytes=40 * 2**20
        ),
    )(x_inner, log_decay.T, in_map.T, out_map.T, grad_out)
    return y, dx, gd.T, d_in.T, d_out.T


def solution(mesh):
    row = ("groups", "dp")
    placed = (P(row, "tensor"), P(row, "tensor"), P(row, None), P(row, None), P(row, "tensor"))
    return jax.shard_map(
        functools.partial(local, mesh.shape["dp"], mesh.shape["tensor"]),
        mesh=mesh,
        in_specs=placed,
        out_specs=(P(row, "tensor"), P(row, "tensor"), P(row, "tensor"), P(row, None), P(row, None)),
        check_vma=False,
    )
```

```python
import functools

import jax
import jax.numpy as jnp
from jax import lax
from jax.experimental import pallas as pl
from jax.experimental.pallas import tpu as pltpu
from jax.sharding import PartitionSpec as P

F32 = jnp.float32
BF16 = jnp.bfloat16
L = 128
PIECES = 4
MESH = pl.DeviceIdType.MESH
HI = lax.Precision.HIGHEST
NN = (((1,), (0,)), ((), ()))
NT = (((1,), (1,)), ((), ()))
TN = (((0,), (0,)), ((), ()))


def dot(a, b, dims=NN, precision=None):
    return lax.dot_general(a, b, dims, precision=precision, preferred_element_type=F32)


def split(a, terms):
    parts = []
    for _ in range(terms):
        part = a.astype(BF16)
        parts.append(part)
        a = a - part.astype(F32)
    return parts


def exact_right(a, ones, dims=NN, terms=3):
    return sum(dot(part, ones, dims) for part in split(a, terms))


def exact_left(ones, a, dims=NN, terms=3):
    return sum(dot(ones, part, dims) for part in split(a, terms))


def iota(shape, dim):
    return lax.broadcasted_iota(jnp.int32, shape, dim)


def ones_where(cond):
    return jnp.where(cond, 1.0, 0.0).astype(BF16)


def kernel(
    hops, peers, heads, x_hbm, ld_hbm, b_hbm, c_hbm, g_hbm,
    yz_ref, small_ref,
    x_ref, ld_ref, b_ref, c_ref, g_ref, load,
    ys, dxs, own, gown, fin, fout, gin, gout, sbd, gbd, pex, mall,
    fsend, frecv, bsend, brecv, msend, mrecv,
):
    rows, width = x_ref.shape
    state = b_ref.shape[0]
    head = width // heads
    chunks = rows // L
    per = heads // PIECES
    wide = per * head
    loads = [
        pltpu.make_async_copy(src, dst, load.at[i])
        for i, (src, dst) in enumerate(
            [(ld_hbm, ld_ref), (b_hbm, b_ref), (c_hbm, c_ref), (x_hbm, x_ref), (g_hbm, g_ref)]
        )
    ]
    for copy in loads:
        copy.start()
    place = lax.axis_index("dp")
    mine = lax.axis_index("tensor")

    barrier = pltpu.get_barrier_semaphore()
    for d in range(1, peers):
        pl.semaphore_signal(
            barrier, inc=1, device_id={"tensor": lax.rem(mine + d, peers)}, device_id_type=MESH
        )

    @pl.when(place > 0)
    def _():
        pl.semaphore_signal(barrier, inc=1, device_id={"dp": place - 1}, device_id_type=MESH)

    @pl.when(place < hops - 1)
    def _():
        pl.semaphore_signal(barrier, inc=1, device_id={"dp": place + 1}, device_id_type=MESH)

    causal = iota((L, L), 0) >= iota((L, L), 1)
    tril = ones_where(causal)
    upper = ones_where(iota((L, L), 0) <= iota((L, L), 1))
    by_col = ones_where(iota((heads, width), 0) == iota((heads, width), 1) // head)
    by_state = ones_where(iota((heads, heads * state), 0) == iota((heads, heads * state), 1) // state)
    tile = ones_where(iota((state, per * state), 0) == iota((state, per * state), 1) % state)
    quad = 4 * head

    for copy in loads:
        copy.wait()
    cum, cum_t, e_exp, t_exp, ce, be, b_t, c_t = [], [], [], [], [], [], [], []
    for c in range(chunks):
        at = pl.ds(c * L, L)
        cu = exact_left(tril, ld_ref[:, at], NT)
        cut = exact_right(ld_ref[:, at], upper)
        cum.append(cu)
        cum_t.append(cut)
        bt = b_ref[:, at]
        ct = c_ref[:, at]
        b_t.append(bt)
        c_t.append(ct)
        pex[c] = jnp.exp(exact_right(cu[L - 8:, :], by_col))
        et = jnp.exp(cut)
        tt = jnp.exp(cut[:, L - 1:] - cut)
        for k in range(width // quad):
            lanes = pl.ds(k * quad, quad)
            lhs_b = jnp.concatenate([bt * tt[h:h + 1, :] for h in range(4 * k, 4 * k + 4)], 0).astype(BF16)
            lhs_c = jnp.concatenate([ct * et[h:h + 1, :] for h in range(4 * k, 4 * k + 4)], 0).astype(BF16)
            rb = dot(lhs_b, x_ref[at, lanes])
            rc = dot(lhs_c, g_ref[at, lanes])
            which = iota((state, quad), 1) // head
            ob = rb[:state]
            oc = rc[:state]
            for h in range(1, 4):
                ob = jnp.where(which == h, rb[h * state:(h + 1) * state], ob)
                oc = jnp.where(which == h, rc[h * state:(h + 1) * state], oc)
            own[c, k * quad // wide, :, (k * quad) % wide:(k * quad) % wide + quad] = ob
            gown[c, k * quad // wide, :, (k * quad) % wide:(k * quad) % wide + quad] = oc

    pl.semaphore_wait(
        barrier, peers - 1 + jnp.minimum(place, 1) + jnp.minimum(hops - 1 - place, 1)
    )

    def decay(c, k):
        return pex[c, 7:8, k * wide:(k + 1) * wide]

    def f_copy(k):
        return pltpu.make_async_remote_copy(
            src_ref=fout.at[k], dst_ref=fin.at[k], send_sem=fsend.at[k], recv_sem=frecv.at[k],
            device_id={"dp": place + 1}, device_id_type=MESH,
        )

    def b_copy(k):
        return pltpu.make_async_remote_copy(
            src_ref=gout.at[k], dst_ref=gin.at[k], send_sem=bsend.at[k], recv_sem=brecv.at[k],
            device_id={"dp": place - 1}, device_id_type=MESH,
        )

    def relay(first):
        for k in range(PIECES):
            @pl.when(place == 0 if first else place > 0)
            def _():
                if first:
                    fin[k] = jnp.zeros(fin.shape[1:], F32)
                else:
                    f_copy(k).wait_recv()

            @pl.when(place < hops - 1)
            def _():
                s = own[0, k] if first else decay(0, k) * fin[k] + own[0, k]
                for c in range(1, chunks):
                    s = decay(c, k) * s + own[c, k]
                fout[k] = s
                f_copy(k).start()

    def relay_back(first):
        for k in range(PIECES):
            @pl.when(place == hops - 1 if first else place < hops - 1)
            def _():
                if first:
                    gin[k] = jnp.zeros(gin.shape[1:], F32)
                else:
                    b_copy(k).wait_recv()

            @pl.when(place > 0)
            def _():
                last = chunks - 1
                s = gown[last, k] if first else decay(last, k) * gin[k] + gown[last, k]
                for c in range(chunks - 2, -1, -1):
                    s = decay(c, k) * s + gown[c, k]
                gout[k] = s
                b_copy(k).start()

    stages = min(hops, 4)
    from_end = hops - 1 - place

    def exchange(stage):
        when = (lambda v: v >= stage) if stage == stages - 1 else (lambda v: v == stage)

        @pl.when(when(place))
        def _():
            relay(stage == 0)

        @pl.when(when(from_end))
        def _():
            relay_back(stage == 0)

    exchange(0)

    scores, grad_scores = [], []
    for c in range(chunks):
        at = pl.ds(c * L, L)
        s = dot(c_t[c], b_t[c], TN, HI)
        scores.append(jnp.where(causal, s, 0.0))
        grad_scores.append(jnp.zeros((L, L), F32))
        ct8 = exact_right(c_t[c], tile, TN)
        bt8 = exact_right(b_t[c], tile, TN)
        cue = exact_right(cum[c], by_state)
        ee = jnp.exp(cue)
        te = jnp.exp(cue[L - 1:, :] - cue)
        e_exp.append(ee)
        t_exp.append(te)
        lanes = per * state
        ce.append([(ct8 * ee[:, k * lanes:(k + 1) * lanes]).astype(BF16) for k in range(PIECES)])
        be.append([(bt8 * te[:, k * lanes:(k + 1) * lanes]).astype(BF16) for k in range(PIECES)])

    pair = 2 * head
    left = ones_where(iota((L, pair), 1) < head)
    right = ones_where(iota((L, pair), 1) >= head)
    units = [(c, p) for p in range(width // pair) for c in range(chunks)]
    for n, (c, p) in enumerate(units):
        for stage in range(1, stages):
            if n == len(units) * stage // (stages - 1) - 1 and stage < stages - 1:
                exchange(stage)
        at = pl.ds(c * L, L)
        lanes = pl.ds(p * pair, pair)
        weights = []
        for h in (2 * p, 2 * p + 1):
            diff = cum[c][:, h:h + 1] - cum_t[c][h:h + 1, :]
            weights.append(jnp.exp(jnp.minimum(diff, 0.0)))
        mix = [(w * scores[c]).astype(BF16) for w in weights]
        x = x_ref[at, lanes]
        g = g_ref[at, lanes]
        x2 = jnp.concatenate([x * left, x * right], 0)
        g2 = jnp.concatenate([g * left, g * right], 0)
        ys[at, lanes] = dot(jnp.concatenate(mix, 1), x2)
        dxs[at, lanes] = dot(jnp.concatenate(mix, 0), g2, TN)
        dm = dot(g, x2, NT)
        grad_scores[c] += weights[0] * dm[:, :L] + weights[1] * dm[:, L:]
    if stages > 1:
        exchange(stages - 1)

    block = ones_where(iota((per * state, wide), 0) // state == iota((per * state, wide), 1) // head)
    acc_c = [jnp.zeros((L, per * state), F32) for _ in range(chunks)]
    acc_b = [jnp.zeros((L, per * state), F32) for _ in range(chunks)]
    ends = []
    for k in range(PIECES):
        states = [fin[k]]
        for c in range(chunks):
            states.append(decay(c, k) * states[c] + own[c, k])
        grads = [gin[k]]
        for c in range(chunks - 1, 0, -1):
            grads.append(decay(c, k) * grads[-1] + gown[c, k])
        grads = grads[::-1]
        ends.append([jnp.sum(grads[c] * states[c + 1], 0, keepdims=True) for c in range(chunks)])
        for c in range(chunks):
            at = pl.ds(c * L, L)
            cols = pl.ds(k * wide, wide)
            lanes = slice(k * per * state, (k + 1) * per * state)
            s2 = jnp.concatenate([states[c].astype(BF16)] * per, 0) * block
            r2 = jnp.concatenate([grads[c].astype(BF16)] * per, 0) * block
            sbd[c, k] = s2
            gbd[c, k] = r2
            acc_c[c] += dot(g_ref[at, cols], s2, NT) * e_exp[c][:, lanes]
            acc_b[c] += dot(x_ref[at, cols], r2, NT) * t_exp[c][:, lanes]

    for c in range(chunks):
        ds = jnp.where(causal, grad_scores[c], 0.0)
        mall[mine, :state, c * L:(c + 1) * L] = exact_left(tile, acc_c[c], NT) + dot(b_t[c], ds, NT, HI)
        mall[mine, state:, c * L:(c + 1) * L] = exact_left(tile, acc_b[c], NT) + dot(c_t[c], ds, NN, HI)

    def m_copy(d, slot):
        return pltpu.make_async_remote_copy(
            src_ref=mall.at[mine], dst_ref=mall.at[slot], send_sem=msend.at[d - 1], recv_sem=mrecv.at[d - 1],
            device_id={"tensor": lax.rem(mine + d, peers)}, device_id_type=MESH,
        )

    for d in range(1, peers):
        m_copy(d, mine).start()

    for c in range(chunks):
        at = pl.ds(c * L, L)
        dcum = jnp.zeros((heads, L), F32)
        for k in range(PIECES):
            cols = pl.ds(k * wide, wide)
            y = ys[at, cols] + dot(ce[c][k], sbd[c, k])
            dx = dxs[at, cols] + dot(be[c][k], gbd[c, k])
            yz_ref[0, at, cols] = y.astype(BF16)
            yz_ref[1, at, cols] = dx.astype(BF16)
            q = g_ref[at, cols].astype(F32) * y - x_ref[at, cols].astype(F32) * dx
            q += jnp.where(iota((L, wide), 0) == L - 1, ends[k][c], 0.0)
            dcum += exact_left(by_col[:, k * wide:(k + 1) * wide], q, NT, 2)
        small_ref[2 * state:, at] = exact_right(dcum, tril)

    for d in range(1, peers):
        m_copy(d, lax.rem(mine + peers - d, peers)).wait_recv()
        m_copy(d, mine).wait_send()
    total = mall[0]
    for d in range(1, peers):
        total += mall[d]
    small_ref[:2 * state] = total

    @pl.when(place < hops - 1)
    def _():
        for k in range(PIECES):
            f_copy(k).wait_send()

    @pl.when(place > 0)
    def _():
        for k in range(PIECES):
            b_copy(k).wait_send()


def local(hops, peers, x_inner, log_decay, in_map, out_map, grad_out):
    rows, width = x_inner.shape
    heads = log_decay.shape[1]
    state = in_map.shape[1]
    chunks = rows // L
    wide = width // PIECES
    piece = (PIECES, state, wide)
    vm = pl.BlockSpec(memory_space=pltpu.VMEM)
    yz, small = pl.pallas_call(
        functools.partial(kernel, hops, peers, heads),
        out_shape=(
            jax.ShapeDtypeStruct((2, rows, width), BF16),
            jax.ShapeDtypeStruct((2 * state + heads, rows), F32),
        ),
        in_specs=[pl.BlockSpec(memory_space=pltpu.HBM)] * 5,
        out_specs=(vm,) * 2,
        scratch_shapes=[
            pltpu.VMEM((rows, width), BF16),
            pltpu.VMEM((heads, rows), F32),
            pltpu.VMEM((state, rows), F32),
            pltpu.VMEM((state, rows), F32),
            pltpu.VMEM((rows, width), BF16),
            pltpu.SemaphoreType.DMA((5,)),
            pltpu.VMEM((rows, width), F32),
            pltpu.VMEM((rows, width), F32),
            pltpu.VMEM((chunks,) + piece, F32),
            pltpu.VMEM((chunks,) + piece, F32),
            pltpu.VMEM(piece, F32),
            pltpu.VMEM(piece, F32),
            pltpu.VMEM(piece, F32),
            pltpu.VMEM(piece, F32),
            pltpu.VMEM((chunks, PIECES, heads // PIECES * state, wide), BF16),
            pltpu.VMEM((chunks, PIECES, heads // PIECES * state, wide), BF16),
            pltpu.VMEM((chunks, 8, width), F32),
            pltpu.VMEM((peers, 2 * state, rows), F32),
            pltpu.SemaphoreType.DMA((PIECES,)),
            pltpu.SemaphoreType.DMA((PIECES,)),
            pltpu.SemaphoreType.DMA((PIECES,)),
            pltpu.SemaphoreType.DMA((PIECES,)),
            pltpu.SemaphoreType.DMA((peers - 1,)),
            pltpu.SemaphoreType.DMA((peers - 1,)),
        ],
        compiler_params=pltpu.CompilerParams(
            collective_id=0, has_side_effects=True, vmem_limit_bytes=40 * 2**20
        ),
    )(*[pltpu.with_memory_space_constraint(a, pltpu.HBM) for a in (x_inner, log_decay.T, in_map.T, out_map.T, grad_out)])
    return yz[0], yz[1], small[2 * state:].T, small[state:2 * state].T, small[:state].T


def solution(mesh):
    row = ("groups", "dp")
    placed = (P(row, "tensor"), P(row, "tensor"), P(row, None), P(row, None), P(row, "tensor"))
    return jax.shard_map(
        functools.partial(local, mesh.shape["dp"], mesh.shape["tensor"]),
        mesh=mesh,
        in_specs=placed,
        out_specs=(P(row, "tensor"), P(row, "tensor"), P(row, "tensor"), P(row, None), P(row, None)),
        check_vma=False,
    )
```

```python
import functools

import jax
import jax.numpy as jnp
from jax import lax
from jax.experimental import pallas as pl
from jax.experimental.pallas import tpu as pltpu
from jax.sharding import PartitionSpec as P

F32 = jnp.float32
BF16 = jnp.bfloat16
L = 128
PIECES = 4
MESH = pl.DeviceIdType.MESH
HI = lax.Precision.HIGHEST
NN = (((1,), (0,)), ((), ()))
NT = (((1,), (1,)), ((), ()))
TN = (((0,), (0,)), ((), ()))


def dot(a, b, dims=NN, precision=None):
    return lax.dot_general(a, b, dims, precision=precision, preferred_element_type=F32)


def split(a, terms):
    parts = []
    for _ in range(terms):
        part = a.astype(BF16)
        parts.append(part)
        a = a - part.astype(F32)
    return parts


def exact_right(a, ones, dims=NN, terms=3):
    return sum(dot(part, ones, dims) for part in split(a, terms))


def exact_left(ones, a, dims=NN, terms=3):
    return sum(dot(ones, part, dims) for part in split(a, terms))


def iota(shape, dim):
    return lax.broadcasted_iota(jnp.int32, shape, dim)


def ones_where(cond):
    return jnp.where(cond, 1.0, 0.0).astype(BF16)


def kernel(
    hops, peers, heads, x_hbm, ld_hbm, b_hbm, c_hbm, g_hbm,
    yz_ref, small_ref,
    x_ref, ld_ref, b_ref, c_ref, g_ref, load,
    ys, dxs, own, gown, fin, fout, gin, gout, sbd, gbd, pex, mall,
    fsend, frecv, bsend, brecv, msend, mrecv,
    ffar, ffar_in, bfar, bfar_in, fsend2, frecv2, bsend2, brecv2,
):
    rows, width = x_ref.shape
    state = b_ref.shape[0]
    head = width // heads
    chunks = rows // L
    per = heads // PIECES
    wide = per * head
    loads = [
        pltpu.make_async_copy(src, dst, load.at[i])
        for i, (src, dst) in enumerate(
            [(ld_hbm, ld_ref), (b_hbm, b_ref), (c_hbm, c_ref), (x_hbm, x_ref), (g_hbm, g_ref)]
        )
    ]
    for copy in loads:
        copy.start()
    place = lax.axis_index("dp")
    mine = lax.axis_index("tensor")

    barrier = pltpu.get_barrier_semaphore()
    for d in range(1, peers):
        pl.semaphore_signal(
            barrier, inc=1, device_id={"tensor": lax.rem(mine + d, peers)}, device_id_type=MESH
        )

    short = hops == 4
    if short:
        for d in range(1, hops):
            pl.semaphore_signal(
                barrier, inc=1, device_id={"dp": lax.rem(place + d, hops)}, device_id_type=MESH
            )
        near = hops - 1
    else:
        near = jnp.minimum(place, 1) + jnp.minimum(hops - 1 - place, 1)

        @pl.when(place > 0)
        def _():
            pl.semaphore_signal(barrier, inc=1, device_id={"dp": place - 1}, device_id_type=MESH)

        @pl.when(place < hops - 1)
        def _():
            pl.semaphore_signal(barrier, inc=1, device_id={"dp": place + 1}, device_id_type=MESH)

    causal = iota((L, L), 0) >= iota((L, L), 1)
    tril = ones_where(causal)
    upper = ones_where(iota((L, L), 0) <= iota((L, L), 1))
    by_col = ones_where(iota((heads, width), 0) == iota((heads, width), 1) // head)
    by_state = ones_where(iota((heads, heads * state), 0) == iota((heads, heads * state), 1) // state)
    tile = ones_where(iota((state, per * state), 0) == iota((state, per * state), 1) % state)
    quad = 4 * head

    for copy in loads[:3]:
        copy.wait()
    cum, cum_t, e_exp, t_exp, ce, be, b_t, c_t = [], [], [], [], [], [], [], []
    for c in range(chunks):
        at = pl.ds(c * L, L)
        cu = exact_left(tril, ld_ref[:, at], NT)
        cut = exact_right(ld_ref[:, at], upper)
        cum.append(cu)
        cum_t.append(cut)
        bt = b_ref[:, at]
        ct = c_ref[:, at]
        b_t.append(bt)
        c_t.append(ct)
        pex[c] = jnp.exp(exact_right(cu[L - 8:, :], by_col))
    pl.semaphore_wait(barrier, peers - 1 + near)
    for copy in loads[3:]:
        copy.wait()

    def decay(c, k):
        return pex[c, 7:8, k * wide:(k + 1) * wide]

    def f_copy(k):
        return pltpu.make_async_remote_copy(
            src_ref=fout.at[k], dst_ref=fin.at[k], send_sem=fsend.at[k], recv_sem=frecv.at[k],
            device_id={"dp": place + 1}, device_id_type=MESH,
        )

    def b_copy(k):
        return pltpu.make_async_remote_copy(
            src_ref=gout.at[k], dst_ref=gin.at[k], send_sem=bsend.at[k], recv_sem=brecv.at[k],
            device_id={"dp": place - 1}, device_id_type=MESH,
        )

    def send(k):
        s = decay(0, k) * fin[k] + own[0, k]
        for c in range(1, chunks):
            s = decay(c, k) * s + own[c, k]
        fout[k] = s
        f_copy(k).start()

    def send_back(k):
        s = decay(chunks - 1, k) * gin[k] + gown[chunks - 1, k]
        for c in range(chunks - 2, -1, -1):
            s = decay(c, k) * s + gown[c, k]
        gout[k] = s
        b_copy(k).start()

    stages = max(min(hops, 4), 2)
    from_end = hops - 1 - place

    def forth(stage, k):
        last = stage == stages - 1

        @pl.when(place >= stage if last else place == stage)
        def _():
            if stage:
                f_copy(k).wait_recv()
            else:
                fin[k] = jnp.zeros(fin.shape[1:], F32)
            pl.when(place < hops - 1)(lambda: send(k))

    def back(stage, k):
        last = stage == stages - 1

        @pl.when(from_end >= stage if last else from_end == stage)
        def _():
            if stage:
                b_copy(k).wait_recv()
            else:
                gin[k] = jnp.zeros(gin.shape[1:], F32)
            pl.when(place > 0)(lambda: send_back(k))

    def two_step(forward):
        if forward:
            at, out, into, mine_own, order = place, fout, fin, own, range(chunks)
            far, far_in, sems = ffar, ffar_in, (fsend, frecv, fsend2, frecv2)
        else:
            at, out, into, mine_own, order = from_end, gout, gin, gown, range(chunks - 1, -1, -1)
            far, far_in, sems = bfar, bfar_in, (bsend, brecv, bsend2, brecv2)
        send_sem, recv_sem, send2_sem, recv2_sem = sems

        def link(src, dst, sent, got, to, k):
            return pltpu.make_async_remote_copy(
                src_ref=src.at[k], dst_ref=dst.at[k], send_sem=sent.at[k], recv_sem=got.at[k],
                device_id={"dp": to if forward else hops - 1 - to}, device_id_type=MESH,
            )

        def total(k, before=None):
            value = before
            for c in order:
                value = mine_own[c, k] if value is None else decay(c, k) * value + mine_own[c, k]
            return value

        def step(stage, k):
            if stage == 0:
                @pl.when(at == 0)
                def _():
                    into[k] = jnp.zeros(into.shape[1:], F32)
                    out[k] = total(k)
                    link(out, into, send_sem, recv_sem, 1, k).start()

                @pl.when(at == 2)
                def _():
                    through = decay(0, k)
                    for c in range(1, chunks):
                        through = through * decay(c, k)
                    far[k, :state] = total(k)
                    far[k, state:] = jnp.broadcast_to(through, (8, wide))
                    link(far, far_in, send2_sem, recv2_sem, 3, k).start()

            if stage == 1:
                @pl.when(at == 1)
                def _():
                    link(out, into, send_sem, recv_sem, 2, k).wait_recv()
                    out[k] = total(k, into[k])
                    link(out, into, send2_sem, recv_sem, 3, k).start()
                    link(out, into, send_sem, recv_sem, 2, k).start()

            if stage == 2:
                @pl.when(at >= 2)
                def _():
                    link(out, into, send_sem, recv_sem, 1, k).wait_recv()

                @pl.when(at == 3)
                def _():
                    link(far, far_in, send2_sem, recv2_sem, 3, k).wait_recv()
                    into[k] = far_in[k, state:state + 1] * into[k] + far_in[k, :state]

        def sent():
            for k in range(PIECES):
                @pl.when(at <= 1)
                def _():
                    link(out, into, send_sem, recv_sem, 2, k).wait_send()

                @pl.when(at == 1)
                def _():
                    link(out, into, send2_sem, recv_sem, 3, k).wait_send()

                @pl.when(at == 2)
                def _():
                    link(far, far_in, send2_sem, recv2_sem, 3, k).wait_send()

        return step, sent

    if short:
        stages = 3
        forth, forth_sent = two_step(True)
        back, back_sent = two_step(False)

    which = iota((state, quad), 1) // head
    e_t = [jnp.exp(cut) for cut in cum_t]
    s_t = [jnp.exp(cut[:, L - 1:] - cut) for cut in cum_t]

    def own_part(scaled, by, values, heads_of):
        lhs = jnp.concatenate([scaled * by[h:h + 1, :] for h in heads_of], 0).astype(BF16)
        r = dot(lhs, values)
        out = r[:state]
        for h in range(1, 4):
            out = jnp.where(which == h, r[h * state:(h + 1) * state], out)
        return out

    def own_piece(k, into, scaled, by, values):
        for c in range(chunks):
            for j in range(0, wide, quad):
                first = (k * wide + j) // head
                part = values[c * L:(c + 1) * L, k * wide + j:k * wide + j + quad]
                into[c, k, :, j:j + quad] = own_part(scaled[c], by[c], part, range(first, first + 4))

    for k in range(PIECES):
        own_piece(k, gown, c_t, e_t, g_ref)
        back(0, k)
    for k in range(PIECES):
        own_piece(k, own, b_t, s_t, x_ref)
        forth(0, k)

    scores, grad_scores = [], []
    for c in range(chunks):
        at = pl.ds(c * L, L)
        s = dot(c_t[c], b_t[c], TN, HI)
        scores.append(jnp.where(causal, s, 0.0))
        grad_scores.append(jnp.zeros((L, L), F32))
        ct8 = exact_right(c_t[c], tile, TN)
        bt8 = exact_right(b_t[c], tile, TN)
        cue = exact_right(cum[c], by_state)
        ee = jnp.exp(cue)
        te = jnp.exp(cue[L - 1:, :] - cue)
        e_exp.append(ee)
        t_exp.append(te)
        lanes = per * state
        ce.append([(ct8 * ee[:, k * lanes:(k + 1) * lanes]).astype(BF16) for k in range(PIECES)])
        be.append([(bt8 * te[:, k * lanes:(k + 1) * lanes]).astype(BF16) for k in range(PIECES)])

    pair = 2 * head
    left = ones_where(iota((L, pair), 1) < head)
    right = ones_where(iota((L, pair), 1) >= head)
    units = [(c, p) for p in range(width // pair) for c in range(chunks)]
    def between(n):
        for stage in range(1, stages - 1):
            if n == (4 if stage == 1 else 24):
                for k in range(PIECES):
                    back(stage, k)
                for k in range(PIECES):
                    forth(stage, k)

    for n, (c, p) in enumerate(units):
        between(n)
        at = pl.ds(c * L, L)
        lanes = pl.ds(p * pair, pair)
        weights = []
        for h in (2 * p, 2 * p + 1):
            diff = cum[c][:, h:h + 1] - cum_t[c][h:h + 1, :]
            weights.append(jnp.exp(jnp.minimum(diff, 0.0)))
        mix = [(w * scores[c]).astype(BF16) for w in weights]
        x = x_ref[at, lanes]
        g = g_ref[at, lanes]
        x2 = jnp.concatenate([x * left, x * right], 0)
        g2 = jnp.concatenate([g * left, g * right], 0)
        ys[at, lanes] = dot(jnp.concatenate(mix, 1), x2)
        dxs[at, lanes] = dot(jnp.concatenate(mix, 0), g2, TN)
        dm = dot(g, x2, NT)
        grad_scores[c] += weights[0] * dm[:, :L] + weights[1] * dm[:, L:]
    between(len(units))

    block = ones_where(iota((per * state, wide), 0) // state == iota((per * state, wide), 1) // head)
    acc_c = [jnp.zeros((L, per * state), F32) for _ in range(chunks)]
    acc_b = [jnp.zeros((L, per * state), F32) for _ in range(chunks)]
    dcum = [jnp.zeros((heads, L), F32) for _ in range(chunks)]
    ends = []

    def finish(k):
        for c in range(chunks):
            at = pl.ds(c * L, L)
            cols = pl.ds(k * wide, wide)
            y = ys[at, cols] + dot(ce[c][k], sbd[c, k])
            dx = dxs[at, cols] + dot(be[c][k], gbd[c, k])
            yz_ref[0, at, cols] = y.astype(BF16)
            yz_ref[1, at, cols] = dx.astype(BF16)
            q = g_ref[at, cols].astype(F32) * y - x_ref[at, cols].astype(F32) * dx
            q += jnp.where(iota((L, wide), 0) == L - 1, ends[k][c], 0.0)
            dcum[c] += exact_left(by_col[:, k * wide:(k + 1) * wide], q, NT, 2)

    for k in range(PIECES):
        back(stages - 1, k)
        forth(stages - 1, k)
        states = [fin[k]]
        for c in range(chunks):
            states.append(decay(c, k) * states[c] + own[c, k])
        grads = [gin[k]]
        for c in range(chunks - 1, 0, -1):
            grads.append(decay(c, k) * grads[-1] + gown[c, k])
        grads = grads[::-1]
        ends.append([jnp.sum(grads[c] * states[c + 1], 0, keepdims=True) for c in range(chunks)])
        for c in range(chunks):
            at = pl.ds(c * L, L)
            cols = pl.ds(k * wide, wide)
            lanes = slice(k * per * state, (k + 1) * per * state)
            s2 = jnp.concatenate([states[c].astype(BF16)] * per, 0) * block
            r2 = jnp.concatenate([grads[c].astype(BF16)] * per, 0) * block
            sbd[c, k] = s2
            gbd[c, k] = r2
            acc_c[c] += dot(g_ref[at, cols], s2, NT) * e_exp[c][:, lanes]
            acc_b[c] += dot(x_ref[at, cols], r2, NT) * t_exp[c][:, lanes]
        if k:
            finish(k - 1)

    for c in range(chunks):
        ds = jnp.where(causal, grad_scores[c], 0.0)
        mall[mine, :state, c * L:(c + 1) * L] = exact_left(tile, acc_c[c], NT) + dot(b_t[c], ds, NT, HI)
        mall[mine, state:, c * L:(c + 1) * L] = exact_left(tile, acc_b[c], NT) + dot(c_t[c], ds, NN, HI)

    def m_copy(d, slot):
        return pltpu.make_async_remote_copy(
            src_ref=mall.at[mine], dst_ref=mall.at[slot], send_sem=msend.at[d - 1], recv_sem=mrecv.at[d - 1],
            device_id={"tensor": lax.rem(mine + d, peers)}, device_id_type=MESH,
        )

    for d in range(1, peers):
        m_copy(d, mine).start()

    finish(PIECES - 1)
    for c in range(chunks):
        small_ref[2 * state:, c * L:(c + 1) * L] = exact_right(dcum[c], tril)

    for d in range(1, peers):
        m_copy(d, lax.rem(mine + peers - d, peers)).wait_recv()
        m_copy(d, mine).wait_send()
    total = mall[0]
    for d in range(1, peers):
        total += mall[d]
    small_ref[:2 * state] = total

    if short:
        forth_sent()
        back_sent()
        return

    @pl.when(place < hops - 1)
    def _():
        for k in range(PIECES):
            f_copy(k).wait_send()

    @pl.when(place > 0)
    def _():
        for k in range(PIECES):
            b_copy(k).wait_send()


def local(hops, peers, x_inner, log_decay, in_map, out_map, grad_out):
    rows, width = x_inner.shape
    heads = log_decay.shape[1]
    state = in_map.shape[1]
    chunks = rows // L
    wide = width // PIECES
    piece = (PIECES, state, wide)
    vm = pl.BlockSpec(memory_space=pltpu.VMEM)
    yz, small = pl.pallas_call(
        functools.partial(kernel, hops, peers, heads),
        out_shape=(
            jax.ShapeDtypeStruct((2, rows, width), BF16),
            jax.ShapeDtypeStruct((2 * state + heads, rows), F32),
        ),
        in_specs=[pl.BlockSpec(memory_space=pltpu.HBM)] * 5,
        out_specs=(vm,) * 2,
        scratch_shapes=[
            pltpu.VMEM((rows, width), BF16),
            pltpu.VMEM((heads, rows), F32),
            pltpu.VMEM((state, rows), F32),
            pltpu.VMEM((state, rows), F32),
            pltpu.VMEM((rows, width), BF16),
            pltpu.SemaphoreType.DMA((5,)),
            pltpu.VMEM((rows, width), F32),
            pltpu.VMEM((rows, width), F32),
            pltpu.VMEM((chunks,) + piece, F32),
            pltpu.VMEM((chunks,) + piece, F32),
            pltpu.VMEM(piece, F32),
            pltpu.VMEM(piece, F32),
            pltpu.VMEM(piece, F32),
            pltpu.VMEM(piece, F32),
            pltpu.VMEM((chunks, PIECES, heads // PIECES * state, wide), BF16),
            pltpu.VMEM((chunks, PIECES, heads // PIECES * state, wide), BF16),
            pltpu.VMEM((chunks, 8, width), F32),
            pltpu.VMEM((peers, 2 * state, rows), F32),
            pltpu.SemaphoreType.DMA((PIECES,)),
            pltpu.SemaphoreType.DMA((PIECES,)),
            pltpu.SemaphoreType.DMA((PIECES,)),
            pltpu.SemaphoreType.DMA((PIECES,)),
            pltpu.SemaphoreType.DMA((peers - 1,)),
            pltpu.SemaphoreType.DMA((peers - 1,)),
            pltpu.VMEM((PIECES, state + 8, wide), F32),
            pltpu.VMEM((PIECES, state + 8, wide), F32),
            pltpu.VMEM((PIECES, state + 8, wide), F32),
            pltpu.VMEM((PIECES, state + 8, wide), F32),
            pltpu.SemaphoreType.DMA((PIECES,)),
            pltpu.SemaphoreType.DMA((PIECES,)),
            pltpu.SemaphoreType.DMA((PIECES,)),
            pltpu.SemaphoreType.DMA((PIECES,)),
        ],
        compiler_params=pltpu.CompilerParams(
            collective_id=0, has_side_effects=True, vmem_limit_bytes=40 * 2**20
        ),
    )(*[pltpu.with_memory_space_constraint(a, pltpu.HBM) for a in (x_inner, log_decay.T, in_map.T, out_map.T, grad_out)])
    return yz[0], yz[1], small[2 * state:].T, small[state:2 * state].T, small[:state].T


def solution(mesh):
    row = ("groups", "dp")
    placed = (P(row, "tensor"), P(row, "tensor"), P(row, None), P(row, None), P(row, "tensor"))
    return jax.shard_map(
        functools.partial(local, mesh.shape["dp"], mesh.shape["tensor"]),
        mesh=mesh,
        in_specs=placed,
        out_specs=(P(row, "tensor"), P(row, "tensor"), P(row, "tensor"), P(row, None), P(row, None)),
        check_vma=False,
    )
```

```python
import functools

import jax
import jax.numpy as jnp
from jax import lax
from jax.experimental import pallas as pl
from jax.experimental.pallas import tpu as pltpu
from jax.sharding import PartitionSpec as P

F32 = jnp.float32
BF16 = jnp.bfloat16
L = 128
PIECES = 4
MESH = pl.DeviceIdType.MESH
HI = lax.Precision.HIGHEST
NN = (((1,), (0,)), ((), ()))
NT = (((1,), (1,)), ((), ()))
TN = (((0,), (0,)), ((), ()))


def dot(a, b, dims=NN, precision=None):
    return lax.dot_general(a, b, dims, precision=precision, preferred_element_type=F32)


def split(a, terms):
    parts = []
    for _ in range(terms):
        part = a.astype(BF16)
        parts.append(part)
        a = a - part.astype(F32)
    return parts


def exact_right(a, ones, dims=NN, terms=3):
    return sum(dot(part, ones, dims) for part in split(a, terms))


def exact_left(ones, a, dims=NN, terms=3):
    return sum(dot(ones, part, dims) for part in split(a, terms))


def iota(shape, dim):
    return lax.broadcasted_iota(jnp.int32, shape, dim)


def ones_where(cond):
    return jnp.where(cond, 1.0, 0.0).astype(BF16)


def kernel(
    hops, peers, heads, x_hbm, ld_hbm, b_hbm, c_hbm, g_hbm,
    yz_ref, small_ref,
    x_ref, ld_ref, b_ref, c_ref, g_ref, load,
    ys, dxs, own, gown, fin, fout, gin, gout, sbd, gbd, pex, mall,
    fsend, frecv, bsend, brecv, msend, mrecv,
    ffar, ffar_in, bfar, bfar_in, fsend2, frecv2, bsend2, brecv2,
):
    rows, width = x_ref.shape
    state = b_ref.shape[0]
    head = width // heads
    chunks = rows // L
    per = heads // PIECES
    wide = per * head
    loads = [
        pltpu.make_async_copy(src, dst, load.at[i])
        for i, (src, dst) in enumerate(
            [(ld_hbm, ld_ref), (b_hbm, b_ref), (c_hbm, c_ref), (g_hbm, g_ref), (x_hbm, x_ref)]
        )
    ]
    for copy in loads:
        copy.start()
    place = lax.axis_index("dp")
    mine = lax.axis_index("tensor")

    barrier = pltpu.get_barrier_semaphore()
    for d in range(1, peers):
        pl.semaphore_signal(
            barrier, inc=1, device_id={"tensor": lax.rem(mine + d, peers)}, device_id_type=MESH
        )

    short = hops == 4
    if short:
        for d in range(1, hops):
            pl.semaphore_signal(
                barrier, inc=1, device_id={"dp": lax.rem(place + d, hops)}, device_id_type=MESH
            )
        near = hops - 1
    else:
        near = jnp.minimum(place, 1) + jnp.minimum(hops - 1 - place, 1)

        @pl.when(place > 0)
        def _():
            pl.semaphore_signal(barrier, inc=1, device_id={"dp": place - 1}, device_id_type=MESH)

        @pl.when(place < hops - 1)
        def _():
            pl.semaphore_signal(barrier, inc=1, device_id={"dp": place + 1}, device_id_type=MESH)

    causal = iota((L, L), 0) >= iota((L, L), 1)
    tril = ones_where(causal)
    upper = ones_where(iota((L, L), 0) <= iota((L, L), 1))
    by_col = ones_where(iota((heads, width), 0) == iota((heads, width), 1) // head)
    by_state = ones_where(iota((heads, heads * state), 0) == iota((heads, heads * state), 1) // state)
    tile = ones_where(iota((state, per * state), 0) == iota((state, per * state), 1) % state)
    quad = 4 * head

    for copy in loads[:3]:
        copy.wait()
    cum, cum_t, e_exp, t_exp, ce, be, b_t, c_t = [], [], [], [], [], [], [], []
    for c in range(chunks):
        at = pl.ds(c * L, L)
        cu = exact_left(tril, ld_ref[:, at], NT)
        cut = exact_right(ld_ref[:, at], upper)
        cum.append(cu)
        cum_t.append(cut)
        bt = b_ref[:, at]
        ct = c_ref[:, at]
        b_t.append(bt)
        c_t.append(ct)
        pex[c] = jnp.exp(exact_right(cu[L - 8:, :], by_col))
    pl.semaphore_wait(barrier, peers - 1 + near)
    loads[3].wait()

    def decay(c, k):
        return pex[c, 7:8, k * wide:(k + 1) * wide]

    def f_copy(k):
        return pltpu.make_async_remote_copy(
            src_ref=fout.at[k], dst_ref=fin.at[k], send_sem=fsend.at[k], recv_sem=frecv.at[k],
            device_id={"dp": place + 1}, device_id_type=MESH,
        )

    def b_copy(k):
        return pltpu.make_async_remote_copy(
            src_ref=gout.at[k], dst_ref=gin.at[k], send_sem=bsend.at[k], recv_sem=brecv.at[k],
            device_id={"dp": place - 1}, device_id_type=MESH,
        )

    def send(k):
        s = decay(0, k) * fin[k] + own[0, k]
        for c in range(1, chunks):
            s = decay(c, k) * s + own[c, k]
        fout[k] = s
        f_copy(k).start()

    def send_back(k):
        s = decay(chunks - 1, k) * gin[k] + gown[chunks - 1, k]
        for c in range(chunks - 2, -1, -1):
            s = decay(c, k) * s + gown[c, k]
        gout[k] = s
        b_copy(k).start()

    stages = max(min(hops, 4), 2)
    from_end = hops - 1 - place

    def forth(stage, k):
        last = stage == stages - 1

        @pl.when(place >= stage if last else place == stage)
        def _():
            if stage:
                f_copy(k).wait_recv()
            else:
                fin[k] = jnp.zeros(fin.shape[1:], F32)
            pl.when(place < hops - 1)(lambda: send(k))

    def back(stage, k):
        last = stage == stages - 1

        @pl.when(from_end >= stage if last else from_end == stage)
        def _():
            if stage:
                b_copy(k).wait_recv()
            else:
                gin[k] = jnp.zeros(gin.shape[1:], F32)
            pl.when(place > 0)(lambda: send_back(k))

    def two_step(forward):
        if forward:
            at, out, into, mine_own, order = place, fout, fin, own, range(chunks)
            far, far_in, sems = ffar, ffar_in, (fsend, frecv, fsend2, frecv2)
        else:
            at, out, into, mine_own, order = from_end, gout, gin, gown, range(chunks - 1, -1, -1)
            far, far_in, sems = bfar, bfar_in, (bsend, brecv, bsend2, brecv2)
        send_sem, recv_sem, send2_sem, recv2_sem = sems

        def link(src, dst, sent, got, to, k):
            return pltpu.make_async_remote_copy(
                src_ref=src.at[k], dst_ref=dst.at[k], send_sem=sent.at[k], recv_sem=got.at[k],
                device_id={"dp": to if forward else hops - 1 - to}, device_id_type=MESH,
            )

        def total(k, before=None):
            value = before
            for c in order:
                value = mine_own[c, k] if value is None else decay(c, k) * value + mine_own[c, k]
            return value

        def step(stage, k):
            if stage == 0:
                @pl.when(at == 0)
                def _():
                    into[k] = jnp.zeros(into.shape[1:], F32)
                    out[k] = total(k)
                    link(out, into, send_sem, recv_sem, 1, k).start()

                @pl.when(at == 2)
                def _():
                    through = decay(0, k)
                    for c in range(1, chunks):
                        through = through * decay(c, k)
                    far[k, :state] = total(k)
                    far[k, state:] = jnp.broadcast_to(through, (8, wide))
                    link(far, far_in, send2_sem, recv2_sem, 3, k).start()

            if stage == 1:
                @pl.when(at == 1)
                def _():
                    link(out, into, send_sem, recv_sem, 2, k).wait_recv()
                    out[k] = total(k, into[k])
                    link(out, into, send2_sem, recv_sem, 3, k).start()
                    link(out, into, send_sem, recv_sem, 2, k).start()

            if stage == 2:
                @pl.when(at >= 2)
                def _():
                    link(out, into, send_sem, recv_sem, 1, k).wait_recv()

                @pl.when(at == 3)
                def _():
                    link(far, far_in, send2_sem, recv2_sem, 3, k).wait_recv()
                    into[k] = far_in[k, state:state + 1] * into[k] + far_in[k, :state]

        def sent():
            for k in range(PIECES):
                @pl.when(at <= 1)
                def _():
                    link(out, into, send_sem, recv_sem, 2, k).wait_send()

                @pl.when(at == 1)
                def _():
                    link(out, into, send2_sem, recv_sem, 3, k).wait_send()

                @pl.when(at == 2)
                def _():
                    link(far, far_in, send2_sem, recv2_sem, 3, k).wait_send()

        return step, sent

    if short:
        stages = 3
        forth, forth_sent = two_step(True)
        back, back_sent = two_step(False)

    which = iota((state, quad), 1) // head
    e_t = [jnp.exp(cut) for cut in cum_t]
    s_t = [jnp.exp(cut[:, L - 1:] - cut) for cut in cum_t]

    def own_part(scaled, by, values, heads_of):
        lhs = jnp.concatenate([scaled * by[h:h + 1, :] for h in heads_of], 0).astype(BF16)
        r = dot(lhs, values)
        out = r[:state]
        for h in range(1, 4):
            out = jnp.where(which == h, r[h * state:(h + 1) * state], out)
        return out

    def own_piece(k, into, scaled, by, values):
        for c in range(chunks):
            for j in range(0, wide, quad):
                first = (k * wide + j) // head
                part = values[c * L:(c + 1) * L, k * wide + j:k * wide + j + quad]
                into[c, k, :, j:j + quad] = own_part(scaled[c], by[c], part, range(first, first + 4))

    for k in range(PIECES):
        own_piece(k, gown, c_t, e_t, g_ref)
        back(0, k)
    loads[4].wait()
    for k in range(PIECES):
        own_piece(k, own, b_t, s_t, x_ref)
        forth(0, k)

    scores, grad_scores = [], []
    for c in range(chunks):
        at = pl.ds(c * L, L)
        s = dot(c_t[c], b_t[c], TN, HI)
        scores.append(jnp.where(causal, s, 0.0))
        grad_scores.append(jnp.zeros((L, L), F32))
        ct8 = exact_right(c_t[c], tile, TN)
        bt8 = exact_right(b_t[c], tile, TN)
        cue = exact_right(cum[c], by_state)
        ee = jnp.exp(cue)
        te = jnp.exp(cue[L - 1:, :] - cue)
        e_exp.append(ee)
        t_exp.append(te)
        lanes = per * state
        ce.append([(ct8 * ee[:, k * lanes:(k + 1) * lanes]).astype(BF16) for k in range(PIECES)])
        be.append([(bt8 * te[:, k * lanes:(k + 1) * lanes]).astype(BF16) for k in range(PIECES)])

    pair = 2 * head
    left = ones_where(iota((L, pair), 1) < head)
    right = ones_where(iota((L, pair), 1) >= head)
    units = [(c, p) for p in range(width // pair) for c in range(chunks)]
    def between(n):
        for stage in range(1, stages - 1):
            if n == (0 if stage == 1 else 24):
                for k in range(PIECES):
                    back(stage, k)
                for k in range(PIECES):
                    forth(stage, k)

    for n, (c, p) in enumerate(units):
        between(n)
        at = pl.ds(c * L, L)
        lanes = pl.ds(p * pair, pair)
        weights = []
        for h in (2 * p, 2 * p + 1):
            diff = cum[c][:, h:h + 1] - cum_t[c][h:h + 1, :]
            weights.append(jnp.exp(jnp.minimum(diff, 0.0)))
        mix = [(w * scores[c]).astype(BF16) for w in weights]
        x = x_ref[at, lanes]
        g = g_ref[at, lanes]
        x2 = jnp.concatenate([x * left, x * right], 0)
        g2 = jnp.concatenate([g * left, g * right], 0)
        ys[at, lanes] = dot(jnp.concatenate(mix, 1), x2)
        dxs[at, lanes] = dot(jnp.concatenate(mix, 0), g2, TN)
        dm = dot(g, x2, NT)
        grad_scores[c] += weights[0] * dm[:, :L] + weights[1] * dm[:, L:]
    between(len(units))

    block = ones_where(iota((per * state, wide), 0) // state == iota((per * state, wide), 1) // head)
    acc_c = [jnp.zeros((L, per * state), F32) for _ in range(chunks)]
    acc_b = [jnp.zeros((L, per * state), F32) for _ in range(chunks)]
    dcum = [jnp.zeros((heads, L), F32) for _ in range(chunks)]
    ends = []

    def finish(k):
        for c in range(chunks):
            at = pl.ds(c * L, L)
            cols = pl.ds(k * wide, wide)
            y = ys[at, cols] + dot(ce[c][k], sbd[c, k])
            dx = dxs[at, cols] + dot(be[c][k], gbd[c, k])
            yz_ref[0, at, cols] = y.astype(BF16)
            yz_ref[1, at, cols] = dx.astype(BF16)
            q = g_ref[at, cols].astype(F32) * y - x_ref[at, cols].astype(F32) * dx
            q += jnp.where(iota((L, wide), 0) == L - 1, ends[k][c], 0.0)
            dcum[c] += exact_left(by_col[:, k * wide:(k + 1) * wide], q, NT, 2)

    for k in range(PIECES):
        back(stages - 1, k)
        forth(stages - 1, k)
        states = [fin[k]]
        for c in range(chunks):
            states.append(decay(c, k) * states[c] + own[c, k])
        grads = [gin[k]]
        for c in range(chunks - 1, 0, -1):
            grads.append(decay(c, k) * grads[-1] + gown[c, k])
        grads = grads[::-1]
        ends.append([jnp.sum(grads[c] * states[c + 1], 0, keepdims=True) for c in range(chunks)])
        for c in range(chunks):
            at = pl.ds(c * L, L)
            cols = pl.ds(k * wide, wide)
            lanes = slice(k * per * state, (k + 1) * per * state)
            s2 = jnp.concatenate([states[c].astype(BF16)] * per, 0) * block
            r2 = jnp.concatenate([grads[c].astype(BF16)] * per, 0) * block
            sbd[c, k] = s2
            gbd[c, k] = r2
            acc_c[c] += dot(g_ref[at, cols], s2, NT) * e_exp[c][:, lanes]
            acc_b[c] += dot(x_ref[at, cols], r2, NT) * t_exp[c][:, lanes]
        if k:
            finish(k - 1)

    for c in range(chunks):
        ds = jnp.where(causal, grad_scores[c], 0.0)
        mall[mine, :state, c * L:(c + 1) * L] = exact_left(tile, acc_c[c], NT) + dot(b_t[c], ds, NT, HI)
        mall[mine, state:, c * L:(c + 1) * L] = exact_left(tile, acc_b[c], NT) + dot(c_t[c], ds, NN, HI)

    def m_copy(d, slot):
        return pltpu.make_async_remote_copy(
            src_ref=mall.at[mine], dst_ref=mall.at[slot], send_sem=msend.at[d - 1], recv_sem=mrecv.at[d - 1],
            device_id={"tensor": lax.rem(mine + d, peers)}, device_id_type=MESH,
        )

    for d in range(1, peers):
        m_copy(d, mine).start()

    finish(PIECES - 1)
    for c in range(chunks):
        small_ref[2 * state:, c * L:(c + 1) * L] = exact_right(dcum[c], tril)

    for d in range(1, peers):
        m_copy(d, lax.rem(mine + peers - d, peers)).wait_recv()
        m_copy(d, mine).wait_send()
    total = mall[0]
    for d in range(1, peers):
        total += mall[d]
    small_ref[:2 * state] = total

    if short:
        forth_sent()
        back_sent()
        return

    @pl.when(place < hops - 1)
    def _():
        for k in range(PIECES):
            f_copy(k).wait_send()

    @pl.when(place > 0)
    def _():
        for k in range(PIECES):
            b_copy(k).wait_send()


def local(hops, peers, x_inner, log_decay, in_map, out_map, grad_out):
    rows, width = x_inner.shape
    heads = log_decay.shape[1]
    state = in_map.shape[1]
    chunks = rows // L
    wide = width // PIECES
    piece = (PIECES, state, wide)
    vm = pl.BlockSpec(memory_space=pltpu.VMEM)
    yz, small = pl.pallas_call(
        functools.partial(kernel, hops, peers, heads),
        out_shape=(
            jax.ShapeDtypeStruct((2, rows, width), BF16),
            jax.ShapeDtypeStruct((2 * state + heads, rows), F32),
        ),
        in_specs=[pl.BlockSpec(memory_space=pltpu.HBM)] * 5,
        out_specs=(vm,) * 2,
        scratch_shapes=[
            pltpu.VMEM((rows, width), BF16),
            pltpu.VMEM((heads, rows), F32),
            pltpu.VMEM((state, rows), F32),
            pltpu.VMEM((state, rows), F32),
            pltpu.VMEM((rows, width), BF16),
            pltpu.SemaphoreType.DMA((5,)),
            pltpu.VMEM((rows, width), F32),
            pltpu.VMEM((rows, width), F32),
            pltpu.VMEM((chunks,) + piece, F32),
            pltpu.VMEM((chunks,) + piece, F32),
            pltpu.VMEM(piece, F32),
            pltpu.VMEM(piece, F32),
            pltpu.VMEM(piece, F32),
            pltpu.VMEM(piece, F32),
            pltpu.VMEM((chunks, PIECES, heads // PIECES * state, wide), BF16),
            pltpu.VMEM((chunks, PIECES, heads // PIECES * state, wide), BF16),
            pltpu.VMEM((chunks, 8, width), F32),
            pltpu.VMEM((peers, 2 * state, rows), F32),
            pltpu.SemaphoreType.DMA((PIECES,)),
            pltpu.SemaphoreType.DMA((PIECES,)),
            pltpu.SemaphoreType.DMA((PIECES,)),
            pltpu.SemaphoreType.DMA((PIECES,)),
            pltpu.SemaphoreType.DMA((peers - 1,)),
            pltpu.SemaphoreType.DMA((peers - 1,)),
            pltpu.VMEM((PIECES, state + 8, wide), F32),
            pltpu.VMEM((PIECES, state + 8, wide), F32),
            pltpu.VMEM((PIECES, state + 8, wide), F32),
            pltpu.VMEM((PIECES, state + 8, wide), F32),
            pltpu.SemaphoreType.DMA((PIECES,)),
            pltpu.SemaphoreType.DMA((PIECES,)),
            pltpu.SemaphoreType.DMA((PIECES,)),
            pltpu.SemaphoreType.DMA((PIECES,)),
        ],
        compiler_params=pltpu.CompilerParams(
            collective_id=0, has_side_effects=True, vmem_limit_bytes=40 * 2**20
        ),
    )(*[pltpu.with_memory_space_constraint(a, pltpu.HBM) for a in (x_inner, log_decay.T, in_map.T, out_map.T, grad_out)])
    return yz[0], yz[1], small[2 * state:].T, small[state:2 * state].T, small[:state].T


def solution(mesh):
    row = ("groups", "dp")
    placed = (P(row, "tensor"), P(row, "tensor"), P(row, None), P(row, None), P(row, "tensor"))
    return jax.shard_map(
        functools.partial(local, mesh.shape["dp"], mesh.shape["tensor"]),
        mesh=mesh,
        in_specs=placed,
        out_specs=(P(row, "tensor"), P(row, "tensor"), P(row, "tensor"), P(row, None), P(row, None)),
        check_vma=False,
    )
```
